256 devices in a mesh: kv: 64 (over z, y, core), tp: 4 (over x).
Axes of the slice: x: 4, y: 4, z: 8, core: 2. Of those that a mesh axis runs over, the one named last changes fastest.
Arguments:
- queries: bfloat16 [384, 8192], P('kv', 'tp'), may hold values from -200 to 200
- shared_prefix_keys: bfloat16 [262144, 1024], P('kv', 'tp'), may hold values from -18 to 18
- shared_prefix_values: bfloat16 [262144, 1024], P('kv', 'tp'), may hold values from -6 to 6
- kept: int32 [262144], P('kv'), may hold values 0 or 1
- row_suffix_keys: bfloat16 [384, 512, 1024], P('kv', None, 'tp'), may hold values from -30 to 30
- row_suffix_values: bfloat16 [384, 512, 1024], P('kv', None, 'tp'), may hold values from -6 to 6
- suffix_lengths: int32 [384], P('kv'), may hold values from 2 to 512, as said below
- out_weight: bfloat16 [8192, 8192], P('tp', 'kv'), may hold values from -0.0625 to 0.0625
Outputs:
- projected: bfloat16 [384, 8192], P('tp', 'kv')
The draws below stay inside these ranges and needn't reach their ends.
Inputs may be any that keep to these rules, and one draw needn't show every extreme that they name: `suffix_lengths`: live suffix positions of a row are its first ones; some row has exactly 512.
All inputs are finite; a program needn't handle non-finite values. No bound on the sum of `kept` on one device may be relied on, other than what follows from the above.
Results may differ from the reference program's by a relative error of at most 0.0065.
Values may be sent and summed in bfloat16 or wider, within the bound.
A program may use at most 128 MiB of HBM per device.

```python
import jax
import jax.numpy as jnp
from jax import lax

D = 8192
QUERY_HEADS = 64
KEY_VALUE_HEADS = 8
HEAD_SIZE = 128
PREFIX_PER_SHARD = 4096
ROWS_DEV = 6
SUFFIX_LIMIT = 512
PREFIX_LENGTH = 262144
QUESTION_ROWS = 384


def draw_queries(key, part):
    key = jax.random.fold_in(key, 1)
    drawn_result = jnp.clip(jax.random.normal(key, (QUESTION_ROWS, QUERY_HEADS, HEAD_SIZE), jnp.float32), -6.0, 6.0)
    return drawn_result.reshape(QUESTION_ROWS, QUERY_HEADS * HEAD_SIZE).astype(jnp.bfloat16)


def draw_row_suffix_keys(key, part):
    key = jax.random.fold_in(key, 2)
    drawn_result = jnp.clip(4.8 * jax.random.normal(key, (QUESTION_ROWS, SUFFIX_LIMIT, KEY_VALUE_HEADS, HEAD_SIZE), jnp.float32), -30.0, 30.0)
    return drawn_result.reshape(QUESTION_ROWS, SUFFIX_LIMIT, KEY_VALUE_HEADS * HEAD_SIZE).astype(jnp.bfloat16)


def draw_suffix_lengths(key, part):
    key = jax.random.fold_in(key, 3)
    owners = QUESTION_ROWS // ROWS_DEV
    lower = max(2, SUFFIX_LIMIT // 8)
    caps = jax.random.randint(jax.random.fold_in(key, 1), (owners,), lower, SUFFIX_LIMIT + 1)
    caps = jnp.repeat(caps, ROWS_DEV)
    raw = jax.random.randint(jax.random.fold_in(key, 2), (QUESTION_ROWS,), 0, 1 << 20)
    lengths = 2 + raw % (caps - 1)
    chosen = jax.random.randint(jax.random.fold_in(key, 4), (), 0, QUESTION_ROWS)
    lengths = jnp.where(jnp.arange(QUESTION_ROWS) == chosen, SUFFIX_LIMIT, lengths)
    return lengths.astype(jnp.int32)


def set_ends(entries, own_key, least, largest):
    extent = entries.shape
    place = [jax.random.randint(jax.random.fold_in(own_key, axis), (), 0, extent[axis]) for axis in range(len(extent))]
    entries = entries.at[tuple(place)].set(least)
    longest = extent.index(max(extent))
    place[longest] = (place[longest] + 1) % extent[longest]
    return entries.at[tuple(place)].set(largest)


def levels(rng, extent, shards, least, top_value):
    gain, own = 1.0, jax.random.fold_in(rng, 6)
    for dim, parts in shards:
        draws = jnp.exp(jax.random.uniform(jax.random.fold_in(own, dim), (parts,), jnp.float32, least / len(shards), top_value / len(shards)))
        gain = gain * jnp.repeat(draws, extent[dim] // parts).reshape([-1 if axis == dim else 1 for axis in range(len(extent))])
    return gain


def normal_values(stream_key, shape, scale, bound, pieces=(), held_as=jnp.bfloat16):
    result = jax.random.normal(stream_key, shape, jnp.float32) * scale
    if len(pieces) > 0:
        result = levels(stream_key, shape, pieces, -0.22, 0.18) * result
    return jnp.clip(result, min=-bound, max=bound).astype(held_as)


def setup_inputs(seed: int = 0) -> dict:
    arg_keys = jax.random.split(jax.random.key(seed), 9)
    queries = draw_queries(jax.random.fold_in(arg_keys[8], 71), 0)
    shared_prefix_keys = normal_values(arg_keys[1], (PREFIX_LENGTH, KEY_VALUE_HEADS * HEAD_SIZE), 3.0, 18.0, ((0, 64), (1, 4)))
    shared_prefix_values = normal_values(arg_keys[2], (PREFIX_LENGTH, KEY_VALUE_HEADS * HEAD_SIZE), 1.0, 6.0, ((0, 64), (1, 4)))
    kept = set_ends((jax.random.randint(arg_keys[3], (PREFIX_LENGTH,), 0, 4) < 3).astype(jnp.int32), jax.random.fold_in(arg_keys[3], 1), 0, 1)
    row_suffix_keys = draw_row_suffix_keys(jax.random.fold_in(arg_keys[8], 71), 0)
    row_suffix_values = normal_values(arg_keys[5], (QUESTION_ROWS, SUFFIX_LIMIT, KEY_VALUE_HEADS * HEAD_SIZE), 1.0, 6.0, ((0, 64), (2, 4)))
    suffix_lengths = draw_suffix_lengths(jax.random.fold_in(arg_keys[8], 71), 0)
    out_weight = normal_values(arg_keys[7], (QUERY_HEADS * HEAD_SIZE, D), (QUERY_HEADS * HEAD_SIZE) ** -0.5, 0.0625, ((0, 4), (1, 64)))
    return {"queries": queries, "shared_prefix_keys": shared_prefix_keys, "shared_prefix_values": shared_prefix_values, "kept": kept, "row_suffix_keys": row_suffix_keys, "row_suffix_values": row_suffix_values, "suffix_lengths": suffix_lengths, "out_weight": out_weight}


def partial_block(query_grouped, keys, values, live, scale):
    k3 = keys.astype(jnp.float32)
    v3 = values.astype(jnp.float32)
    scores = jnp.einsum("rhgd,khd->rhgk", query_grouped, k3) * scale
    scores = jnp.where(live, scores, -jnp.inf)
    top = jnp.max(scores, axis=-1)
    weights = jnp.where(live, jnp.exp(scores - top[..., None]), 0.0).astype(jnp.bfloat16)
    wfloat = weights.astype(jnp.float32)
    numer = jnp.einsum("rhgk,khd->rhgd", wfloat, v3)
    denom = jnp.sum(wfloat, axis=-1)
    return numer, top, denom


def reference(queries, shared_prefix_keys, shared_prefix_values, kept, row_suffix_keys, row_suffix_values, suffix_lengths, out_weight):
    scale = HEAD_SIZE ** -0.5
    query_group = QUERY_HEADS // KEY_VALUE_HEADS
    query_grouped = queries.astype(jnp.float32).reshape(QUESTION_ROWS, KEY_VALUE_HEADS, query_group, HEAD_SIZE)
    suffix_key_rows = row_suffix_keys.astype(jnp.float32).reshape(QUESTION_ROWS, SUFFIX_LIMIT, KEY_VALUE_HEADS, HEAD_SIZE)
    suffix_value_rows = row_suffix_values.astype(jnp.float32).reshape(QUESTION_ROWS, SUFFIX_LIMIT, KEY_VALUE_HEADS, HEAD_SIZE)
    scores = jnp.einsum("rhgd,rkhd->rhgk", query_grouped, suffix_key_rows) * scale
    live = (jnp.arange(SUFFIX_LIMIT, dtype=jnp.int32)[None, :] < suffix_lengths[:, None])[:, None, None, :]
    scores = jnp.where(live, scores, -jnp.inf)
    top_s = jnp.max(scores, axis=-1)
    weights = jnp.where(live, jnp.exp(scores - top_s[..., None]), 0.0).astype(jnp.bfloat16).astype(jnp.float32)
    numer_s = jnp.einsum("rhgk,rkhd->rhgd", weights, suffix_value_rows)
    denom_s = jnp.sum(weights, axis=-1)
    block_list = PREFIX_LENGTH // PREFIX_PER_SHARD
    block_keys = shared_prefix_keys.reshape(block_list, PREFIX_PER_SHARD, KEY_VALUE_HEADS, HEAD_SIZE)
    block_values = shared_prefix_values.reshape(block_list, PREFIX_PER_SHARD, KEY_VALUE_HEADS, HEAD_SIZE)
    kept_b = kept.reshape(block_list, PREFIX_PER_SHARD)

    def step(carry, block):
        best, numer, denom = carry
        keys, values, keep = block
        o_b, m_b, l_b = partial_block(query_grouped, keys, values, (keep > 0)[None, None, None, :], scale)
        new = jnp.maximum(best, m_b)
        old_w = jnp.exp(best - new)
        new_w = jnp.exp(m_b - new)
        numer = numer * old_w[..., None] + o_b * new_w[..., None]
        denom = denom * old_w + l_b * new_w
        return (new, numer, denom), None

    (best, numer, denom), _ = lax.scan(step, (top_s, numer_s, denom_s), (block_keys, block_values, kept_b))
    attention = (numer / denom[..., None]).reshape(QUESTION_ROWS, QUERY_HEADS * HEAD_SIZE).astype(jnp.bfloat16)
    return jnp.dot(attention, out_weight, preferred_element_type=jnp.float32).astype(jnp.bfloat16)
```

```python
import jax
import jax.numpy as jnp
from jax import lax
from jax.experimental import pallas as pl
from jax.experimental.pallas import tpu as pltpu
from jax.sharding import PartitionSpec as P

MESH = pl.DeviceIdType.MESH
F32 = jnp.float32
BF16 = jnp.bfloat16
HD = 128
ROWS = 6
G = 8
QV = ROWS * G
KEYS = 4096
SPAN = 512
NZ, NY = 8, 4
HALF = NZ * QV
UNIT = 2 * HALF
TK = 512
VR = 144
C = float(HD**-0.5 * 1.4426950408889634)
DROPPED = -1e30


def merge(parts):
    top = parts[0][1]
    for _, lse in parts[1:]:
        top = jnp.maximum(top, lse)
    total, out = None, None
    for o, lse in parts:
        w = jnp.exp2(lse - top)
        total = w if total is None else total + w
        out = o * w if out is None else out + o * w
    return out * (1.0 / total), top + jnp.log2(total)


def split3(x):
    hi = x.astype(BF16).astype(F32)
    rest = x - hi
    mid = rest.astype(BF16).astype(F32)
    return hi, mid, rest - mid


def pack_t(o, lse):
    n = o.shape[1]
    hi, mid, lo = split3(lse)
    row = lax.broadcasted_iota(jnp.int32, (VR - HD, n), 0)
    stat = jnp.where(row == 0, hi, jnp.where(row == 1, mid, jnp.where(row == 2, lo, 0.0)))
    return jnp.concatenate([o, stat], axis=0).astype(BF16)


def unpack_t(x):
    x = x.astype(F32)
    return x[:HD], x[HD : HD + 1] + x[HD + 1 : HD + 2] + x[HD + 2 : HD + 3]


def unpack_r(x):
    x = x.astype(F32)
    return x[:, :HD], x[:, HD : HD + 1] + x[:, HD + 1 : HD + 2] + x[:, HD + 2 : HD + 3]


def kernel(
    q_ref, k_hbm, v_hbm, kept_ref, sk_hbm, sv_hbm, len_ref, w_hbm, out_ref,
    kbuf, vbuf, vt, bias, s0, s1, skbuf, svbuf, wbuf, qf, qg, rsout, sibin, ysend, yin, zout, zin,
    attg, attf, osuf, lsuf, part, tpin,
    load_sem, qz_s, qz_r, qy_s, qy_r, qs_s, qs_r, sib_s, sib_r, ry_s, ry_r, rz_s, rz_r,
    az_s, az_r, ay_s, ay_r, as_s, as_r, tp_s, tp_r,
):
    k = lax.axis_index("kv")
    x = lax.axis_index("tp")
    z, y, c = k // (2 * NY), (k // 2) % NY, k % 2

    def dev(zz, yy, cc):
        return ((zz * NY + yy) * 2 + cc, x)

    sibling = dev(z, y, 1 - c)

    def remote(src, dst, s, r, to):
        return pltpu.make_async_remote_copy(
            src_ref=src, dst_ref=dst, send_sem=s, recv_sem=r, device_id=to, device_id_type=MESH
        )

    loads = [
        pltpu.make_async_copy(sk_hbm, skbuf, load_sem.at[0]),
        pltpu.make_async_copy(sv_hbm, svbuf, load_sem.at[1]),
    ]
    for h in range(2):
        cols = slice(h * HD, (h + 1) * HD)
        loads.append(pltpu.make_async_copy(v_hbm.at[:, cols], vbuf.at[h], load_sem.at[2 + 2 * h]))
        loads.append(pltpu.make_async_copy(k_hbm.at[:, cols], kbuf.at[h], load_sem.at[3 + 2 * h]))
    loads.append(pltpu.make_async_copy(w_hbm, wbuf, load_sem.at[6]))
    for copy in loads:
        copy.start()

    own = q_ref[...].astype(F32)
    for h in range(2):
        for g in range(G):
            at = (h * G + g) * HD
            qf[h, pl.ds(g, ROWS, stride=G), :] = own[:, at : at + HD]
        qg[h, y, c, z] = qf[h].astype(BF16)

    barrier = pltpu.get_barrier_semaphore()
    peers = [sibling]
    peers += [dev(z, (y + i) % NY, c) for i in range(1, NY)]
    peers += [dev((z + i) % NZ, y, c) for i in range(1, NZ)]
    peers += [(k, (x + i) % 4) for i in range(1, 4)]
    for p in peers:
        pl.semaphore_signal(barrier, inc=1, device_id=p, device_id_type=MESH)
    pl.semaphore_wait(barrier, len(peers))

    def qz(h, i):
        blk = qg.at[h, y, c, z]
        return remote(blk, blk, qz_s.at[h, i], qz_r.at[h, i], dev((z + i) % NZ, y, c))

    def qz_arrival(h, i):
        blk = qg.at[h, y, c, (z + NZ - i) % NZ]
        return remote(blk, blk, qz_s.at[h, i], qz_r.at[h, i], dev((z + i) % NZ, y, c))

    def unit_offset(s):
        j = (s + s // 4) % 4
        return j + (j // 2) * (5 - 2 * j)

    def qy(s):
        blk = qg.at[s // 4, y, c]
        return remote(blk, blk, qy_s.at[s], qy_r.at[s], dev(z, (y + NY - unit_offset(s)) % NY, c))

    def qy_arrival(s):
        blk = qg.at[s // 4, (y + unit_offset(s)) % NY, c]
        return remote(blk, blk, qy_s.at[s], qy_r.at[s], sibling)

    def qs(s):
        blk = qg.at[s // 4, (y + unit_offset(s)) % NY, c]
        return remote(blk, blk, qs_s.at[s], qs_r.at[s], sibling)

    def qs_arrival(s):
        blk = qg.at[s // 4, (y + unit_offset(s)) % NY, 1 - c]
        return remote(blk, blk, qs_s.at[s], qs_r.at[s], sibling)

    def forward(s):
        qy_arrival(s).wait_recv()
        qs(s).start()

    for h in range(2):
        for i in (1, 7, 2, 6, 3, 5, 4):
            qz(h, i).start()

    kept = jnp.where(kept_ref[...] > 0, 0.0, DROPPED).astype(F32)
    kept = jnp.concatenate([kept, jnp.zeros((HD - KEYS // HD, HD), F32)], axis=0).T
    for j in range(KEYS // HD):
        bias[j * HD : (j + 1) * HD, :] = jnp.broadcast_to(kept[:, j : j + 1], (HD, HD)).astype(BF16)

    for h in range(2):
        loads[2 + 2 * h].wait()

        def turn(j, _, h=h):
            at = pl.multiple_of(j * 512, 512)
            vt[h, :HD, pl.ds(at, 512)] = vbuf[h, pl.ds(at, 512), :].astype(F32).T.astype(BF16)
            return 0

        lax.fori_loop(0, KEYS // 512, turn, 0)
        vt[h, HD:, :] = jnp.ones((VR - HD, KEYS), BF16)

    def spread(h):
        for i in range(1, NZ):
            qz_arrival(h, i).wait_recv()
        qs(7 * h).start()
        for s in (1, 2, 3):
            qy(3 * h + s).start()

    spread(0)

    loads[0].wait()
    loads[1].wait()
    for r in range(ROWS):
        live = lax.broadcasted_iota(jnp.int32, (G, SPAN), 1) < len_ref[r]
        for h in range(2):
            cols = slice(h * HD, (h + 1) * HD)
            q8 = qf[h, r * G : (r + 1) * G, :].astype(BF16)
            t = lax.dot_general(q8, skbuf[r, :, cols], (((1,), (1,)), ((), ())), preferred_element_type=F32)
            t = jnp.where(live, t * C, DROPPED)
            top = jnp.max(t, axis=1, keepdims=True)
            p = jnp.exp2(t - top).astype(BF16)
            total = jnp.sum(p.astype(F32), axis=1, keepdims=True)
            o = jnp.dot(p, svbuf[r, :, cols], preferred_element_type=F32)
            osuf[h, r * G : (r + 1) * G, :] = o * (1.0 / total)
            lsuf[h, r * G : (r + 1) * G, :] = jnp.broadcast_to(top + jnp.log2(total), (G, HD))

    spread(1)
    loads[3].wait()
    loads[5].wait()
    forward(1)
    qs_arrival(0).wait_recv()

    first_lane = (lax.broadcasted_iota(jnp.int32, (UNIT, HD), 1) == 0).astype(F32).astype(BF16)

    def unit_queries(s):
        q = qg[s // 4, (y + unit_offset(s)) % NY].reshape(UNIT, HD)
        return jnp.concatenate([q, first_lane], axis=1)

    def scores(s, q, t, buf, m8):
        rows = slice(t * TK, (t + 1) * TK)
        kt = jnp.concatenate([kbuf[s // 4, rows, :], bias[rows, :]], axis=1)
        sc = lax.dot_general(kt, q, (((1,), (1,)), ((), ())), preferred_element_type=F32)
        buf[rows, :] = sc
        return jnp.maximum(m8, jnp.max(sc.reshape(TK // 8, 8, UNIT), axis=0))

    def lowest():
        return jnp.full((8, UNIT), -3e38, F32)

    def stage(s, buf, nxt, m8):
        last = isinstance(s, int) and s == 7
        top = jnp.max(m8, axis=0, keepdims=True) * C
        q = None if last else unit_queries(s + 1)
        o = jnp.zeros((VR, UNIT), F32)
        m_next = lowest()
        for t in range(KEYS // TK):
            if not last:
                m_next = scores(s + 1, q, t, nxt, m_next)
            rows = slice(t * TK, (t + 1) * TK)
            p = jnp.exp2(buf[rows, :] * C - top).astype(BF16)
            o = o + jnp.dot(vt[s // 4, :, rows], p, preferred_element_type=F32)
        total = o[HD : HD + 1]
        done = pack_t(o[:HD] * (1.0 / total), top + jnp.log2(total))
        rsout[s, 0] = done[:, :HALF]
        rsout[s, 1] = done[:, HALF:]
        sib_send(s).start()
        return m_next

    def sib_send(s):
        return remote(rsout.at[s, 1 - c], sibin.at[s], sib_s.at[s], sib_r.at[s], sibling)

    def y_send(s):
        return remote(ysend.at[s], yin.at[s], ry_s.at[s], ry_r.at[s], dev(z, (y + unit_offset(s)) % NY, c))

    def sib_merge(s):
        sib_send(s).wait_recv()
        ysend[s] = pack_t(*merge([unpack_t(rsout[s, c]), unpack_t(sibin[s])]))

    def z_send(h, i):
        to = (z + i) % NZ
        return remote(zout.at[h, to], zin.at[h, i], rz_s.at[h, i], rz_r.at[h, i], dev(to, y, c))

    def y_merge(h):
        parts = [unpack_t(ysend[7 * h])]
        for s in (1, 2, 3):
            y_send(3 * h + s).wait_recv()
            parts.append(unpack_t(yin[3 * h + s]))
        o, lse = merge(parts)
        hi, mid, lo = split3(jnp.broadcast_to(lse, (HD, HALF)).T)
        lane = lax.broadcasted_iota(jnp.int32, (HALF, HD), 1)
        stat = jnp.where(lane == 0, hi, jnp.where(lane == 1, mid, jnp.where(lane == 2, lo, 0.0)))
        zout[h] = jnp.concatenate([o.T, stat], axis=1).astype(BF16).reshape(NZ, QV, 2 * HD)
        for i in (4, 3, 5, 2, 6, 1, 7):
            z_send(h, i).start()

    def az(h, i):
        blk = attg.at[h, z, y, c]
        return remote(blk, blk, az_s.at[h, i], az_r.at[h, i], dev((z + i) % NZ, y, c))

    def az_arrival(h, i):
        blk = attg.at[h, (z + NZ - i) % NZ, y, c]
        return remote(blk, blk, az_s.at[h, i], az_r.at[h, i], dev((z + i) % NZ, y, c))

    def z_merge(h):
        parts = [(osuf[h], lsuf[h][:, :1]), unpack_r(zout[h, z])]
        for i in range(1, NZ):
            z_send(h, i).wait_recv()
            parts.append(unpack_r(zin[h, i]))
        attg[h, z, y, c] = merge(parts)[0].astype(BF16)
        for i in (4, 3, 5, 2, 6, 1, 7):
            az(h, i).start()

    def ay(h, i):
        blk = attg.at[h, :, y, c]
        return remote(blk, blk, ay_s.at[h, i], ay_r.at[h, i], dev(z, (y + NY - i) % NY, c))

    def ay_arrival(h, i):
        blk = attg.at[h, :, (y + i) % NY, c]
        return remote(blk, blk, ay_s.at[h, i], ay_r.at[h, i], sibling)

    def a_sib(h, i):
        blk = attg.at[h, :, (y + i) % NY, c]
        return remote(blk, blk, as_s.at[h, i], as_r.at[h, i], sibling)

    def a_sib_arrival(h, i):
        blk = attg.at[h, :, (y + i) % NY, 1 - c]
        return remote(blk, blk, as_s.at[h, i], as_r.at[h, i], sibling)

    def gather_y(h):
        for i in range(1, NZ):
            az_arrival(h, i).wait_recv()
        for i in (2, 1, 3):
            ay(h, i).start()
        a_sib(h, 0).start()

    def gather_core(h):
        for i in (1, 3, 2):
            ay_arrival(h, i).wait_recv()
            a_sib(h, i).start()

    def project(h):
        for i in range(NY):
            a_sib_arrival(h, i).wait_recv()
        attf[...] = attg[h].reshape(-1, HD).astype(F32)
        rows = NZ * NY * 2 * ROWS
        att = jnp.concatenate([attf[pl.ds(g, rows, stride=G), :].astype(BF16) for g in range(G)], axis=1)
        return jnp.dot(att, wbuf[h * G * HD : (h + 1) * G * HD, :], preferred_element_type=F32)

    q = unit_queries(0)
    m8 = lowest()
    for t in range(KEYS // TK):
        m8 = scores(0, q, t, s0, m8)

    def pair(it, m8):
        a = 2 * it
        b = a + 1
        pl.when(it <= 2)(lambda: forward(a + 2))
        qs_arrival(b).wait_recv()
        m8 = stage(a, s0, s1, m8)

        @pl.when(it >= 1)
        def _():
            sib_merge(a - 1)
            y_send(a - 1).start()

        @pl.when(it == 3)
        def _():
            z_merge(0)

        @pl.when(it <= 1)
        def _():
            forward(b + 2)

        @pl.when(it <= 2)
        def _():
            qs_arrival(a + 2).wait_recv()

        m8 = stage(b, s1, s0, m8)
        sib_merge(a)

        @pl.when(it >= 1)
        def _():
            y_send(a).start()

        @pl.when(it == 2)
        def _():
            y_merge(0)

        return m8

    pair(3, lax.fori_loop(0, 3, pair, m8))

    gather_y(0)
    sib_merge(7)
    y_merge(1)
    gather_core(0)
    loads[6].wait()
    part[...] = project(0)
    z_merge(1)
    gather_y(1)
    gather_core(1)
    part[...] += project(1)

    per = part.shape[0] // 4

    def mine(xx):
        return part.at[pl.ds(pl.multiple_of(xx * per, 8), per), :]

    def tp_send(i):
        to = (x + i) % 4
        return remote(mine(to), tpin.at[i], tp_s.at[i], tp_r.at[i], (k, to))

    for i in range(1, 4):
        tp_send(i).start()
    total = part[pl.ds(pl.multiple_of(x * per, 8), per), :]
    for i in range(1, 4):
        tp_send(i).wait_recv()
        total = total + tpin[i]
    out_ref[...] = total.astype(BF16)

    for h in range(2):
        for i in range(1, NZ):
            qz(h, i).wait_send()
            z_send(h, i).wait_send()
            az(h, i).wait_send()
        for i in range(1, NY):
            ay(h, i).wait_send()
        for i in range(NY):
            a_sib(h, i).wait_send()
    for s in range(8):
        qs(s).wait_send()
        sib_send(s).wait_send()
        if 1 <= s <= 6:
            qy(s).wait_send()
            y_send(s).wait_send()
    for i in range(1, 4):
        tp_send(i).wait_send()


def per_device(queries, keys, values, kept, suffix_keys, suffix_values, lengths, out_weight):
    any_space = pl.BlockSpec(memory_space=pl.ANY)
    vmem = pl.BlockSpec(memory_space=pltpu.VMEM)
    sem = pltpu.SemaphoreType.DMA
    return pl.pallas_call(
        kernel,
        out_shape=jax.ShapeDtypeStruct((96, 128), BF16),
        in_specs=[
            vmem, any_space, any_space, vmem, any_space, any_space,
            pl.BlockSpec(memory_space=pltpu.SMEM), any_space,
        ],
        out_specs=vmem,
        scratch_shapes=[
            pltpu.VMEM((2, KEYS, HD), BF16),
            pltpu.VMEM((2, KEYS, HD), BF16),
            pltpu.VMEM((2, VR, KEYS), BF16),
            pltpu.VMEM((KEYS, HD), BF16),
            pltpu.VMEM((KEYS, UNIT), F32),
            pltpu.VMEM((KEYS, UNIT), F32),
            pltpu.VMEM((ROWS, SPAN, 2 * HD), BF16),
            pltpu.VMEM((ROWS, SPAN, 2 * HD), BF16),
            pltpu.VMEM((2 * G * HD, 128), BF16),
            pltpu.VMEM((2, QV, HD), F32),
            pltpu.VMEM((2, NY, 2, NZ, QV, HD), BF16),
            pltpu.VMEM((8, 2, VR, HALF), BF16),
            pltpu.VMEM((8, VR, HALF), BF16),
            pltpu.VMEM((8, VR, HALF), BF16),
            pltpu.VMEM((8, VR, HALF), BF16),
            pltpu.VMEM((2, NZ, QV, 2 * HD), BF16),
            pltpu.VMEM((2, NZ, QV, 2 * HD), BF16),
            pltpu.VMEM((2, NZ, NY, 2, QV, HD), BF16),
            pltpu.VMEM((NZ * NY * 2 * QV, HD), F32),
            pltpu.VMEM((2, QV, HD), F32),
            pltpu.VMEM((2, QV, HD), F32),
            pltpu.VMEM((384, 128), F32),
            pltpu.VMEM((4, 96, 128), F32),
            sem((7,)),
            sem((2, 8)), sem((2, 8)), sem((8,)), sem((8,)), sem((8,)), sem((8,)),
            sem((8,)), sem((8,)), sem((8,)), sem((8,)), sem((2, 8)), sem((2, 8)),
            sem((2, 8)), sem((2, 8)), sem((2, 4)), sem((2, 4)), sem((2, 4)), sem((2, 4)),
            sem((4,)), sem((4,)),
        ],
        compiler_params=pltpu.CompilerParams(
            collective_id=0, has_side_effects=True, vmem_limit_bytes=60 * 2**20
        ),
    )(queries, keys, values, kept.reshape(-1, 128), suffix_keys, suffix_values, lengths, out_weight)


def solution(mesh):
    return jax.shard_map(
        per_device,
        mesh=mesh,
        in_specs=(
            P("kv", "tp"),
            P("kv", "tp"),
            P("kv", "tp"),
            P("kv"),
            P("kv", None, "tp"),
            P("kv", None, "tp"),
            P("kv"),
            P("tp", "kv"),
        ),
        out_specs=P("tp", "kv"),
        check_vma=False,
    )
```

```python
import jax
import jax.numpy as jnp
from jax import lax
from jax.experimental import pallas as pl
from jax.experimental.pallas import tpu as pltpu
from jax.sharding import PartitionSpec as P

MESH = pl.DeviceIdType.MESH
F32 = jnp.float32
BF16 = jnp.bfloat16
HD = 128
ROWS = 6
G = 8
QV = ROWS * G
KEYS = 4096
SPAN = 512
NZ, NY = 8, 4
HALF = NZ * QV
UNIT = 2 * HALF
TK = 512
VR = 144
C = float(HD**-0.5 * 1.4426950408889634)
DROPPED = -1e30


def merge(parts):
    top = parts[0][1]
    for _, lse in parts[1:]:
        top = jnp.maximum(top, lse)
    total, out = None, None
    for o, lse in parts:
        w = jnp.exp2(lse - top)
        total = w if total is None else total + w
        out = o * w if out is None else out + o * w
    return out * (1.0 / total), top + jnp.log2(total)


def split3(x):
    hi = x.astype(BF16).astype(F32)
    rest = x - hi
    mid = rest.astype(BF16).astype(F32)
    return hi, mid, rest - mid


def pack_t(o, lse):
    n = o.shape[1]
    hi, mid, lo = split3(lse)
    row = lax.broadcasted_iota(jnp.int32, (VR - HD, n), 0)
    stat = jnp.where(row == 0, hi, jnp.where(row == 1, mid, jnp.where(row == 2, lo, 0.0)))
    return jnp.concatenate([o, stat], axis=0).astype(BF16)


def unpack_t(x):
    x = x.astype(F32)
    return x[:HD], x[HD : HD + 1] + x[HD + 1 : HD + 2] + x[HD + 2 : HD + 3]


def kernel(
    q_ref, k_hbm, v_hbm, kept_ref, sk_hbm, sv_hbm, len_ref, w_hbm, out_ref,
    kbuf, vbuf, vt, bias, s0, s1, skbuf, svbuf, wbuf, qf, qg, rsout, sibin, ysend, yin, zout, zin,
    attg, attf, osuf, lsuf, part, half, tpin,
    load_sem, qz_s, qz_r, qy_s, qy_r, qs_s, qs_r, sib_s, sib_r, ry_s, ry_r, rz_s, rz_r,
    az_s, az_r, ay_s, ay_r, as_s, as_r, tp_s, tp_r,
):
    k = lax.axis_index("kv")
    x = lax.axis_index("tp")
    z, y, c = k // (2 * NY), (k // 2) % NY, k % 2

    def dev(zz, yy, cc):
        return ((zz * NY + yy) * 2 + cc, x)

    sibling = dev(z, y, 1 - c)

    def remote(src, dst, s, r, to):
        return pltpu.make_async_remote_copy(
            src_ref=src, dst_ref=dst, send_sem=s, recv_sem=r, device_id=to, device_id_type=MESH
        )

    barrier = pltpu.get_barrier_semaphore()
    peers = [sibling]
    peers += [dev((z + i) % NZ, y, c) for i in (4, 3, 5, 2, 6, 1, 7)]
    peers += [dev(z, (y + i) % NY, c) for i in (2, 1, 3)]
    peers += [(k, (x + i) % 4) for i in range(1, 4)]
    for p in peers:
        pl.semaphore_signal(barrier, inc=1, device_id=p, device_id_type=MESH)

    loads = [
        pltpu.make_async_copy(sk_hbm, skbuf, load_sem.at[0]),
        pltpu.make_async_copy(sv_hbm, svbuf, load_sem.at[1]),
    ]
    for h in range(2):
        cols = slice(h * HD, (h + 1) * HD)
        loads.append(pltpu.make_async_copy(v_hbm.at[:, cols], vbuf.at[h], load_sem.at[2 + 2 * h]))
        loads.append(pltpu.make_async_copy(k_hbm.at[:, cols], kbuf.at[h], load_sem.at[3 + 2 * h]))
    loads.append(pltpu.make_async_copy(w_hbm, wbuf, load_sem.at[6]))
    for i in (2, 4, 0, 1, 3, 5, 6):
        loads[i].start()

    own = q_ref[...].astype(F32)
    for h in range(2):
        for g in range(G):
            at = (h * G + g) * HD
            qf[h, pl.ds(g, ROWS, stride=G), :] = own[:, at : at + HD]
        qg[h, y, c, z] = qf[h].astype(BF16)

    kept = jnp.where(kept_ref[...] > 0, 0.0, DROPPED).astype(F32)
    kept = jnp.concatenate([kept, jnp.zeros((HD - KEYS // HD, HD), F32)], axis=0).T
    for j in range(KEYS // HD):
        bias[j * HD : (j + 1) * HD, :] = jnp.broadcast_to(kept[:, j : j + 1], (HD, HD)).astype(BF16)

    for h in range(2):
        loads[2 + 2 * h].wait()

        def turn(j, _, h=h):
            at = pl.multiple_of(j * 512, 512)
            vt[h, :HD, pl.ds(at, 512)] = vbuf[h, pl.ds(at, 512), :].astype(F32).T.astype(BF16)
            return 0

        lax.fori_loop(0, KEYS // 512, turn, 0)
        vt[h, HD:, :] = jnp.ones((VR - HD, KEYS), BF16)

    pl.semaphore_wait(barrier, len(peers))

    def qz(h, i):
        blk = qg.at[h, y, c, z]
        return remote(blk, blk, qz_s.at[h, i], qz_r.at[h, i], dev((z + i) % NZ, y, c))

    def qz_arrival(h, i):
        blk = qg.at[h, y, c, (z + NZ - i) % NZ]
        return remote(blk, blk, qz_s.at[h, i], qz_r.at[h, i], dev((z + i) % NZ, y, c))

    def unit_offset(s):
        return (s + s // 4) % NY

    def qy(s, zz):
        blk = qg.at[s // 4, y, c, zz]
        return remote(blk, blk, qy_s.at[s], qy_r.at[s], dev(z, (y + NY - unit_offset(s)) % NY, c))

    def qy_all(s):
        blk = qg.at[s // 4, (y + unit_offset(s)) % NY, c]
        return remote(blk, blk, qy_s.at[s], qy_r.at[s], sibling)

    def qs_own(s, zz):
        blk = qg.at[s // 4, y, c, zz]
        return remote(blk, blk, qs_s.at[s], qs_r.at[s], sibling)

    def qs(s):
        blk = qg.at[s // 4, (y + unit_offset(s)) % NY, c]
        return remote(blk, blk, qs_s.at[s], qs_r.at[s], sibling)

    def qs_arrival(s):
        blk = qg.at[s // 4, (y + unit_offset(s)) % NY, 1 - c]
        return remote(blk, blk, qs_s.at[s], qs_r.at[s], sibling)

    def forward(s):
        qy_all(s).wait_recv()
        qs(s).start()

    def relay(h, i):
        if i:
            qz_arrival(h, i).wait_recv()
        zz = (z + NZ - i) % NZ
        qs_own(7 * h, zz).start()
        for s in (1, 3, 2):
            qy(3 * h + s, zz).start()

    def spread(h):
        for i in (4, 3, 5, 2, 6, 1, 7):
            qz(h, i).start()
        relay(h, 0)

    spread(0)

    loads[0].wait()
    loads[1].wait()

    def suffix(r):
        live = lax.broadcasted_iota(jnp.int32, (G, SPAN), 1) < len_ref[r]
        for h in range(2):
            cols = slice(h * HD, (h + 1) * HD)
            q8 = qf[h, r * G : (r + 1) * G, :].astype(BF16)
            t = lax.dot_general(q8, skbuf[r, :, cols], (((1,), (1,)), ((), ())), preferred_element_type=F32)
            t = jnp.where(live, t * C, DROPPED)
            top = jnp.max(t, axis=1, keepdims=True)
            p = jnp.exp2(t - top).astype(BF16)
            total = jnp.sum(p.astype(F32), axis=1, keepdims=True)
            o = jnp.dot(p, svbuf[r, :, cols], preferred_element_type=F32)
            osuf[h, r * G : (r + 1) * G, :] = o * (1.0 / total)
            lsuf[h, r * G : (r + 1) * G, :] = jnp.broadcast_to(top + jnp.log2(total), (G, HD))

    suffix(0)
    suffix(1)
    relay(0, 1)
    relay(0, 7)
    suffix(2)
    suffix(3)
    for i in (2, 6, 3, 5, 4):
        relay(0, i)
    spread(1)
    suffix(4)
    suffix(5)
    loads[3].wait()
    loads[5].wait()
    qs_arrival(0).wait_recv()

    first_lane = (lax.broadcasted_iota(jnp.int32, (UNIT, HD), 1) == 0).astype(F32).astype(BF16)

    def unit_queries(s):
        q = qg[s // 4, (y + unit_offset(s)) % NY].reshape(UNIT, HD)
        return jnp.concatenate([q, first_lane], axis=1)

    def scores(s, q, t, buf, m8):
        rows = slice(t * TK, (t + 1) * TK)
        kt = jnp.concatenate([kbuf[s // 4, rows, :], bias[rows, :]], axis=1)
        sc = lax.dot_general(kt, q, (((1,), (1,)), ((), ())), preferred_element_type=F32)
        buf[rows, :] = sc
        return jnp.maximum(m8, jnp.max(sc.reshape(TK // 8, 8, UNIT), axis=0))

    def lowest():
        return jnp.full((8, UNIT), -3e38, F32)

    def stage(s, buf, nxt, m8):
        top = jnp.max(m8, axis=0, keepdims=True) * C
        q = None if nxt is None else unit_queries(s + 1)
        o = jnp.zeros((VR, UNIT), F32)
        m_next = lowest()
        for t in range(KEYS // TK):
            if nxt is not None:
                m_next = scores(s + 1, q, t, nxt, m_next)
            rows = slice(t * TK, (t + 1) * TK)
            p = jnp.exp2(buf[rows, :] * C - top).astype(BF16)
            o = o + jnp.dot(vt[s // 4, :, rows], p, preferred_element_type=F32)
        total = o[HD : HD + 1]
        done = pack_t(o[:HD] * (1.0 / total), top + jnp.log2(total))
        rsout[s, 0] = done[:, :HALF]
        rsout[s, 1] = done[:, HALF:]
        sib_send(s).start()
        return m_next

    def sib_send(s):
        return remote(rsout.at[s, 1 - c], sibin.at[s], sib_s.at[s], sib_r.at[s], sibling)

    def y_send(s):
        return remote(ysend.at[s], yin.at[s], ry_s.at[s], ry_r.at[s], dev(z, (y + unit_offset(s)) % NY, c))

    def sib_merge(s):
        sib_send(s).wait_recv()
        ysend[s] = pack_t(*merge([unpack_t(rsout[s, c]), unpack_t(sibin[s])]))

    def z_send(h, i):
        to = (z + i) % NZ
        return remote(zout.at[h, to], zin.at[h, i], rz_s.at[h, i], rz_r.at[h, i], dev(to, y, c))

    def y_merge(h):
        parts = [unpack_t(ysend[7 * h])]
        for s in (1, 2, 3):
            y_send(3 * h + s).wait_recv()
            parts.append(unpack_t(yin[3 * h + s]))
        o, lse = merge(parts)
        stat = jnp.concatenate(list(split3(lse)) + [jnp.zeros((13, HALF), F32)], axis=0)
        rows = o.T.astype(BF16)
        for zz in range(NZ):
            zout[h, zz, :QV, :] = rows[zz * QV : (zz + 1) * QV]
            turned = stat if zz == 0 else pltpu.roll(stat, HALF - zz * QV, axis=1)
            zout[h, zz, QV:, :] = turned[:, :HD].astype(BF16)
        for i in (4, 3, 5, 2, 6, 1, 7):
            z_send(h, i).start()

    def az(h, i):
        blk = attg.at[h, z, y, c]
        return remote(blk, blk, az_s.at[h, i], az_r.at[h, i], dev((z + i) % NZ, y, c))

    def az_arrival(h, i):
        blk = attg.at[h, (z + NZ - i) % NZ, y, c]
        return remote(blk, blk, az_s.at[h, i], az_r.at[h, i], dev((z + i) % NZ, y, c))

    def z_merge(h):
        for i in range(1, NZ):
            z_send(h, i).wait_recv()
        got = [zout[h, z]] + [zin[h, i] for i in range(1, NZ)]
        stats = [g[QV:].astype(F32) for g in got]
        lse = jnp.concatenate([st[0:1] + st[1:2] + st[2:3] for st in stats], axis=0).T
        parts = [(g[:QV].astype(F32), lse[:QV, i : i + 1]) for i, g in enumerate(got)]
        parts.append((osuf[h], lsuf[h][:, :1]))
        attg[h, z, y, c] = merge(parts)[0].astype(BF16)
        for i in (4, 3, 5, 2, 6, 1, 7):
            az(h, i).start()
        a_relay(h, 0)

    def ay(h, i, zz):
        blk = attg.at[h, zz, y, c]
        return remote(blk, blk, ay_s.at[h, i], ay_r.at[h, i], dev(z, (y + NY - i) % NY, c))

    def ay_all(h, i):
        blk = attg.at[h, :, (y + i) % NY, c]
        return remote(blk, blk, ay_s.at[h, i], ay_r.at[h, i], sibling)

    def a_own(h, zz):
        blk = attg.at[h, zz, y, c]
        return remote(blk, blk, as_s.at[h, 0], as_r.at[h, 0], sibling)

    def a_sib(h, i):
        blk = attg.at[h, :, (y + i) % NY, c]
        return remote(blk, blk, as_s.at[h, i], as_r.at[h, i], sibling)

    def a_sib_arrival(h, i):
        blk = attg.at[h, :, (y + i) % NY, 1 - c]
        return remote(blk, blk, as_s.at[h, i], as_r.at[h, i], sibling)

    def a_relay(h, i):
        if i:
            az_arrival(h, i).wait_recv()
        zz = (z + NZ - i) % NZ
        for j in (2, 1, 3):
            ay(h, j, zz).start()
        a_own(h, zz).start()

    def gather_y(h):
        for i in (1, 7, 2, 6, 3, 5, 4):
            a_relay(h, i)

    def gather_core(h):
        for i in (1, 3, 2):
            ay_all(h, i).wait_recv()
            a_sib(h, i).start()

    def project(h):
        for i in range(NY):
            a_sib_arrival(h, i).wait_recv()
        attf[...] = attg[h].reshape(-1, HD).astype(F32)
        rows = NZ * NY * 2 * ROWS
        att = jnp.concatenate([attf[pl.ds(g, rows, stride=G), :].astype(BF16) for g in range(G)], axis=1)
        return jnp.dot(att, wbuf[h * G * HD : (h + 1) * G * HD, :], preferred_element_type=F32)

    def all_scores(s, buf):
        q = unit_queries(s)
        m8 = lowest()
        for t in range(KEYS // TK):
            m8 = scores(s, q, t, buf, m8)
        return m8

    m8 = all_scores(0, s0)
    forward(1)
    stage(0, s0, None, m8)
    for i in (1, 7, 2, 6, 3, 5, 4):
        relay(1, i)
    forward(2)
    qs_arrival(1).wait_recv()
    m8 = all_scores(1, s0)

    def pair(it, m8):
        a = 2 * it + 1
        b = a + 1
        qs_arrival(b).wait_recv()
        pl.when(it <= 1)(lambda: forward(b + 1))
        m8 = stage(a, s0, s1, m8)
        sib_merge(a - 1)
        pl.when(it >= 1)(lambda: y_send(a - 1).start())
        qs_arrival(b + 1).wait_recv()
        pl.when(it <= 1)(lambda: forward(b + 2))
        if isinstance(it, int):
            y_merge(0)
        m8 = stage(b, s1, s0, m8)
        sib_merge(a)
        y_send(a).start()
        return m8

    m8 = pair(2, lax.fori_loop(0, 2, pair, m8))
    sib_merge(6)
    y_send(6).start()
    stage(7, s0, None, m8)
    z_merge(0)
    sib_merge(7)
    y_merge(1)
    gather_y(0)
    for h in range(2):
        for i in range(1, NZ):
            qz(h, i).wait_send()
            if h == 0:
                z_send(0, i).wait_send()
    for s in range(8):
        qs(s).wait_send()
        sib_send(s).wait_send()
        if 1 <= s <= 6:
            qy_all(s).wait_send()
            y_send(s).wait_send()
    loads[6].wait()
    z_merge(1)
    gather_core(0)
    part[...] = project(0)
    gather_y(1)
    for h in range(2):
        for i in range(1, NZ):
            az(h, i).wait_send()
            if h == 1:
                z_send(1, i).wait_send()
    gather_core(1)
    part[...] += project(1)
    half[...] = part[...].astype(BF16)

    per = part.shape[0] // 4

    def mine(xx):
        return half.at[pl.ds(pl.multiple_of(xx * per, 32), per), :]

    def tp_send(i):
        to = (x + i) % 4
        return remote(mine(to), tpin.at[i], tp_s.at[i], tp_r.at[i], (k, to))

    for i in range(1, 4):
        tp_send(i).start()
    for h in range(2):
        for i in range(1, NY):
            ay_all(h, i).wait_send()
        for i in range(NY):
            a_sib(h, i).wait_send()
    total = part[pl.ds(pl.multiple_of(x * per, 8), per), :]
    for i in range(1, 4):
        tp_send(i).wait_recv()
        total = total + tpin[i].astype(F32)
    out_ref[...] = total.astype(BF16)
    for i in range(1, 4):
        tp_send(i).wait_send()


def per_device(queries, keys, values, kept, suffix_keys, suffix_values, lengths, out_weight):
    any_space = pl.BlockSpec(memory_space=pl.ANY)
    vmem = pl.BlockSpec(memory_space=pltpu.VMEM)
    sem = pltpu.SemaphoreType.DMA
    return pl.pallas_call(
        kernel,
        out_shape=jax.ShapeDtypeStruct((96, 128), BF16),
        in_specs=[
            vmem, any_space, any_space, vmem, any_space, any_space,
            pl.BlockSpec(memory_space=pltpu.SMEM), any_space,
        ],
        out_specs=vmem,
        scratch_shapes=[
            pltpu.VMEM((2, KEYS, HD), BF16),
            pltpu.VMEM((2, KEYS, HD), BF16),
            pltpu.VMEM((2, VR, KEYS), BF16),
            pltpu.VMEM((KEYS, HD), BF16),
            pltpu.VMEM((KEYS, UNIT), F32),
            pltpu.VMEM((KEYS, UNIT), F32),
            pltpu.VMEM((ROWS, SPAN, 2 * HD), BF16),
            pltpu.VMEM((ROWS, SPAN, 2 * HD), BF16),
            pltpu.VMEM((2 * G * HD, 128), BF16),
            pltpu.VMEM((2, QV, HD), F32),
            pltpu.VMEM((2, NY, 2, NZ, QV, HD), BF16),
            pltpu.VMEM((8, 2, VR, HALF), BF16),
            pltpu.VMEM((8, VR, HALF), BF16),
            pltpu.VMEM((8, VR, HALF), BF16),
            pltpu.VMEM((8, VR, HALF), BF16),
            pltpu.VMEM((2, NZ, QV + 16, HD), BF16),
            pltpu.VMEM((2, NZ, QV + 16, HD), BF16),
            pltpu.VMEM((2, NZ, NY, 2, QV, HD), BF16),
            pltpu.VMEM((NZ * NY * 2 * QV, HD), F32),
            pltpu.VMEM((2, QV, HD), F32),
            pltpu.VMEM((2, QV, HD), F32),
            pltpu.VMEM((384, 128), F32),
            pltpu.VMEM((384, 128), BF16),
            pltpu.VMEM((4, 96, 128), BF16),
            sem((7,)),
            sem((2, 8)), sem((2, 8)), sem((8,)), sem((8,)), sem((8,)), sem((8,)),
            sem((8,)), sem((8,)), sem((8,)), sem((8,)), sem((2, 8)), sem((2, 8)),
            sem((2, 8)), sem((2, 8)), sem((2, 4)), sem((2, 4)), sem((2, 4)), sem((2, 4)),
            sem((4,)), sem((4,)),
        ],
        compiler_params=pltpu.CompilerParams(
            collective_id=0, has_side_effects=True, vmem_limit_bytes=60 * 2**20
        ),
    )(queries, keys, values, kept.reshape(-1, 128), suffix_keys, suffix_values, lengths, out_weight)


def solution(mesh):
    return jax.shard_map(
        per_device,
        mesh=mesh,
        in_specs=(
            P("kv", "tp"),
            P("kv", "tp"),
            P("kv", "tp"),
            P("kv"),
            P("kv", None, "tp"),
            P("kv", None, "tp"),
            P("kv"),
            P("tp", "kv"),
        ),
        out_specs=P("tp", "kv"),
        check_vma=False,
    )
```

```python
import jax
import jax.numpy as jnp
from jax import lax
from jax.experimental import pallas as pl
from jax.experimental.pallas import tpu as pltpu
from jax.sharding import PartitionSpec as P

MESH = pl.DeviceIdType.MESH
F32 = jnp.float32
BF16 = jnp.bfloat16
HD = 128
ROWS = 6
G = 8
QV = ROWS * G
KEYS = 4096
SPAN = 512
NZ, NY = 8, 4
HALF = NZ * QV
UNIT = 2 * HALF
TK = 512
VR = 144
C = float(HD**-0.5 * 1.4426950408889634)
DROPPED = -1e30


def merge(parts):
    top = parts[0][1]
    for _, lse in parts[1:]:
        top = jnp.maximum(top, lse)
    total, out = None, None
    for o, lse in parts:
        w = jnp.exp2(lse - top)
        total = w if total is None else total + w
        out = o * w if out is None else out + o * w
    return out * (1.0 / total), top + jnp.log2(total)


def split3(x):
    hi = x.astype(BF16).astype(F32)
    rest = x - hi
    mid = rest.astype(BF16).astype(F32)
    return hi, mid, rest - mid


def pack_t(o, lse):
    n = o.shape[1]
    hi, mid, lo = split3(lse)
    row = lax.broadcasted_iota(jnp.int32, (VR - HD, n), 0)
    stat = jnp.where(row == 0, hi, jnp.where(row == 1, mid, jnp.where(row == 2, lo, 0.0)))
    return jnp.concatenate([o, stat], axis=0).astype(BF16)


def unpack_t(x):
    x = x.astype(F32)
    return x[:HD], x[HD : HD + 1] + x[HD + 1 : HD + 2] + x[HD + 2 : HD + 3]


def kernel(
    q_ref, k_hbm, v_hbm, kept_ref, sk_hbm, sv_hbm, len_ref, w_hbm, out_ref,
    kbuf, vbuf, vt, bias, s0, s1, skbuf, svbuf, wbuf, qf, qg, rsout, sibin, ysend, yin, zout, zin,
    attg, attf, osuf, lsuf, part, half, tpin,
    load_sem, qz_s, qz_r, qy_s, qy_r, qs_s, qs_r, sib_s, sib_r, ry_s, ry_r, rz_s, rz_r,
    az_s, az_r, ay_s, ay_r, as_s, as_r, tp_s, tp_r,
):
    k = lax.axis_index("kv")
    x = lax.axis_index("tp")
    z, y, c = k // (2 * NY), (k // 2) % NY, k % 2

    def dev(zz, yy, cc):
        return ((zz * NY + yy) * 2 + cc, x)

    sibling = dev(z, y, 1 - c)

    def remote(src, dst, s, r, to):
        return pltpu.make_async_remote_copy(
            src_ref=src, dst_ref=dst, send_sem=s, recv_sem=r, device_id=to, device_id_type=MESH
        )

    barrier = pltpu.get_barrier_semaphore()
    peers = [sibling]
    peers += [dev((z + i) % NZ, y, c) for i in (4, 3, 5, 2, 6, 1, 7)]
    peers += [dev(z, (y + i) % NY, c) for i in (2, 1, 3)]
    peers += [(k, (x + i) % 4) for i in range(1, 4)]
    for p in peers:
        pl.semaphore_signal(barrier, inc=1, device_id=p, device_id_type=MESH)

    loads = [
        pltpu.make_async_copy(sk_hbm, skbuf, load_sem.at[0]),
        pltpu.make_async_copy(sv_hbm, svbuf, load_sem.at[1]),
    ]
    for h in range(2):
        cols = slice(h * HD, (h + 1) * HD)
        loads.append(pltpu.make_async_copy(v_hbm.at[:, cols], vbuf.at[h], load_sem.at[2 + 2 * h]))
        loads.append(pltpu.make_async_copy(k_hbm.at[:, cols], kbuf.at[h], load_sem.at[3 + 2 * h]))
    loads.append(pltpu.make_async_copy(w_hbm, wbuf, load_sem.at[6]))
    for i in (2, 4, 0, 1, 3, 5, 6):
        loads[i].start()

    own = q_ref[...].astype(F32)
    for h in range(2):
        for g in range(G):
            at = (h * G + g) * HD
            qf[h, pl.ds(g, ROWS, stride=G), :] = own[:, at : at + HD]
        qg[h, y, c, z] = qf[h].astype(BF16)

    kept = jnp.where(kept_ref[...] > 0, 0.0, DROPPED).astype(F32)
    kept = jnp.concatenate([kept, jnp.zeros((HD - KEYS // HD, HD), F32)], axis=0).T
    for j in range(KEYS // HD):
        bias[j * HD : (j + 1) * HD, :] = jnp.broadcast_to(kept[:, j : j + 1], (HD, HD)).astype(BF16)

    for h in range(2):
        loads[2 + 2 * h].wait()

        def turn(j, _, h=h):
            at = pl.multiple_of(j * 512, 512)
            vt[h, :HD, pl.ds(at, 512)] = vbuf[h, pl.ds(at, 512), :].astype(F32).T.astype(BF16)
            return 0

        lax.fori_loop(0, KEYS // 512, turn, 0)
        vt[h, HD:, :] = jnp.ones((VR - HD, KEYS), BF16)

    pl.semaphore_wait(barrier, len(peers))

    def qz(h, i):
        blk = qg.at[h, y, c, z]
        return remote(blk, blk, qz_s.at[h, i], qz_r.at[h, i], dev((z + i) % NZ, y, c))

    def qz_arrival(h, i):
        blk = qg.at[h, y, c, (z + NZ - i) % NZ]
        return remote(blk, blk, qz_s.at[h, i], qz_r.at[h, i], dev((z + i) % NZ, y, c))

    def unit_offset(s):
        return (s + s // 4) % NY

    def qy(s, zz):
        blk = qg.at[s // 4, y, c, zz]
        return remote(blk, blk, qy_s.at[s], qy_r.at[s], dev(z, (y + NY - unit_offset(s)) % NY, c))

    def qy_all(s):
        blk = qg.at[s // 4, (y + unit_offset(s)) % NY, c]
        return remote(blk, blk, qy_s.at[s], qy_r.at[s], sibling)

    def qs_own(s, zz):
        blk = qg.at[s // 4, y, c, zz]
        return remote(blk, blk, qs_s.at[s], qs_r.at[s], sibling)

    def qs(s):
        blk = qg.at[s // 4, (y + unit_offset(s)) % NY, c]
        return remote(blk, blk, qs_s.at[s], qs_r.at[s], sibling)

    def qs_arrival(s):
        blk = qg.at[s // 4, (y + unit_offset(s)) % NY, 1 - c]
        return remote(blk, blk, qs_s.at[s], qs_r.at[s], sibling)

    def forward(s):
        qy_all(s).wait_recv()
        qs(s).start()

    def relay(h, i):
        if i:
            qz_arrival(h, i).wait_recv()
        zz = (z + NZ - i) % NZ
        qs_own(7 * h, zz).start()
        for s in (1, 3):
            qy(3 * h + s, zz).start()

    def qy_far(h):
        blk = qg.at[h, y, c]
        s = 3 * h + 2
        return remote(blk, blk, qy_s.at[s], qy_r.at[s], dev(z, (y + 2) % NY, c))

    def spread(h):
        for i in (4, 3, 5, 2, 6, 1, 7):
            qz(h, i).start()
        relay(h, 0)

    spread(0)

    loads[0].wait()
    loads[1].wait()

    def suffix(r):
        live = lax.broadcasted_iota(jnp.int32, (G, SPAN), 1) < len_ref[r]
        for h in range(2):
            cols = slice(h * HD, (h + 1) * HD)
            q8 = qf[h, r * G : (r + 1) * G, :].astype(BF16)
            t = lax.dot_general(q8, skbuf[r, :, cols], (((1,), (1,)), ((), ())), preferred_element_type=F32)
            t = jnp.where(live, t * C, DROPPED)
            top = jnp.max(t, axis=1, keepdims=True)
            p = jnp.exp2(t - top).astype(BF16)
            total = jnp.sum(p.astype(F32), axis=1, keepdims=True)
            o = jnp.dot(p, svbuf[r, :, cols], preferred_element_type=F32)
            osuf[h, r * G : (r + 1) * G, :] = o * (1.0 / total)
            lsuf[h, r * G : (r + 1) * G, :] = jnp.broadcast_to(top + jnp.log2(total), (G, HD))

    suffix(0)
    suffix(1)
    relay(0, 1)
    relay(0, 7)
    suffix(2)
    suffix(3)
    for i in (2, 6, 3, 5, 4):
        relay(0, i)
    qy_far(0).start()
    spread(1)
    suffix(4)
    suffix(5)
    loads[3].wait()
    loads[5].wait()
    qs_arrival(0).wait_recv()

    first_lane = (lax.broadcasted_iota(jnp.int32, (UNIT, HD), 1) == 0).astype(F32).astype(BF16)

    def unit_queries(s):
        q = qg[s // 4, (y + unit_offset(s)) % NY].reshape(UNIT, HD)
        return jnp.concatenate([q, first_lane], axis=1)

    def scores(s, q, t, buf, m8):
        rows = slice(t * TK, (t + 1) * TK)
        kt = jnp.concatenate([kbuf[s // 4, rows, :], bias[rows, :]], axis=1)
        sc = lax.dot_general(kt, q, (((1,), (1,)), ((), ())), preferred_element_type=F32)
        buf[rows, :] = sc
        return jnp.maximum(m8, jnp.max(sc.reshape(TK // 8, 8, UNIT), axis=0))

    def lowest():
        return jnp.full((8, UNIT), -3e38, F32)

    def stage(s, buf, nxt, m8):
        top = jnp.max(m8, axis=0, keepdims=True) * C
        q = None if nxt is None else unit_queries(s + 1)
        o = jnp.zeros((VR, UNIT), F32)
        m_next = lowest()
        for t in range(KEYS // TK):
            if nxt is not None:
                m_next = scores(s + 1, q, t, nxt, m_next)
            rows = slice(t * TK, (t + 1) * TK)
            p = jnp.exp2(buf[rows, :] * C - top).astype(BF16)
            o = o + jnp.dot(vt[s // 4, :, rows], p, preferred_element_type=F32)
        total = o[HD : HD + 1]
        done = pack_t(o[:HD] * (1.0 / total), top + jnp.log2(total))
        rsout[s, 0] = done[:, :HALF]
        rsout[s, 1] = done[:, HALF:]
        sib_send(s).start()
        return m_next

    def sib_send(s):
        return remote(rsout.at[s, 1 - c], sibin.at[s], sib_s.at[s], sib_r.at[s], sibling)

    def y_send(s):
        return remote(ysend.at[s], yin.at[s], ry_s.at[s], ry_r.at[s], dev(z, (y + unit_offset(s)) % NY, c))

    def sib_merge(s):
        sib_send(s).wait_recv()
        ysend[s] = pack_t(*merge([unpack_t(rsout[s, c]), unpack_t(sibin[s])]))

    def z_send(h, i):
        to = (z + i) % NZ
        return remote(zout.at[h, to], zin.at[h, i], rz_s.at[h, i], rz_r.at[h, i], dev(to, y, c))

    def y_merge(h):
        parts = [unpack_t(ysend[7 * h])]
        for s in (1, 2, 3):
            y_send(3 * h + s).wait_recv()
            parts.append(unpack_t(yin[3 * h + s]))
        o, lse = merge(parts)
        stat = jnp.concatenate(list(split3(lse)) + [jnp.zeros((13, HALF), F32)], axis=0)
        rows = o.T.astype(BF16)
        for zz in range(NZ):
            zout[h, zz, :QV, :] = rows[zz * QV : (zz + 1) * QV]
            turned = stat if zz == 0 else pltpu.roll(stat, HALF - zz * QV, axis=1)
            zout[h, zz, QV:, :] = turned[:, :HD].astype(BF16)
        for i in (4, 3, 5, 2, 6, 1, 7):
            z_send(h, i).start()

    def az(h, i):
        blk = attg.at[h, z, y, c]
        return remote(blk, blk, az_s.at[h, i], az_r.at[h, i], dev((z + i) % NZ, y, c))

    def az_arrival(h, i):
        blk = attg.at[h, (z + NZ - i) % NZ, y, c]
        return remote(blk, blk, az_s.at[h, i], az_r.at[h, i], dev((z + i) % NZ, y, c))

    def z_merge(h):
        for i in range(1, NZ):
            z_send(h, i).wait_recv()
        got = [zout[h, z]] + [zin[h, i] for i in range(1, NZ)]
        stats = [g[QV:].astype(F32) for g in got]
        lse = jnp.concatenate([st[0:1] + st[1:2] + st[2:3] for st in stats], axis=0).T
        parts = [(g[:QV].astype(F32), lse[:QV, i : i + 1]) for i, g in enumerate(got)]
        parts.append((osuf[h], lsuf[h][:, :1]))
        attg[h, z, y, c] = merge(parts)[0].astype(BF16)
        for i in (4, 3, 5, 2, 6, 1, 7):
            az(h, i).start()
        a_relay(h, 0)

    def ay(h, i, zz):
        blk = attg.at[h, zz, y, c]
        return remote(blk, blk, ay_s.at[h, i], ay_r.at[h, i], dev(z, (y + NY - i) % NY, c))

    def ay_all(h, i):
        blk = attg.at[h, :, (y + i) % NY, c]
        return remote(blk, blk, ay_s.at[h, i], ay_r.at[h, i], sibling)

    def a_own(h, zz):
        blk = attg.at[h, zz, y, c]
        return remote(blk, blk, as_s.at[h, 0], as_r.at[h, 0], sibling)

    def a_sib(h, i):
        blk = attg.at[h, :, (y + i) % NY, c]
        return remote(blk, blk, as_s.at[h, i], as_r.at[h, i], sibling)

    def a_sib_arrival(h, i):
        blk = attg.at[h, :, (y + i) % NY, 1 - c]
        return remote(blk, blk, as_s.at[h, i], as_r.at[h, i], sibling)

    def a_relay(h, i):
        if i:
            az_arrival(h, i).wait_recv()
        zz = (z + NZ - i) % NZ
        for j in (2, 1, 3):
            ay(h, j, zz).start()
        a_own(h, zz).start()

    def gather_y(h):
        for i in (1, 7, 2, 6, 3, 5, 4):
            a_relay(h, i)

    def gather_core(h):
        for i in (1, 3, 2):
            ay_all(h, i).wait_recv()
            a_sib(h, i).start()

    def project(h):
        for i in range(NY):
            a_sib_arrival(h, i).wait_recv()
        attf[...] = attg[h].reshape(-1, HD).astype(F32)
        rows = NZ * NY * 2 * ROWS
        att = jnp.concatenate([attf[pl.ds(g, rows, stride=G), :].astype(BF16) for g in range(G)], axis=1)
        return jnp.dot(att, wbuf[h * G * HD : (h + 1) * G * HD, :], preferred_element_type=F32)

    def all_scores(s, buf):
        q = unit_queries(s)
        m8 = lowest()
        for t in range(KEYS // TK):
            m8 = scores(s, q, t, buf, m8)
        return m8

    m8 = all_scores(0, s0)
    forward(1)
    stage(0, s0, None, m8)
    for i in (1, 7, 2, 6, 3, 5, 4):
        relay(1, i)
    qy_far(1).start()
    forward(2)
    qs_arrival(1).wait_recv()
    m8 = all_scores(1, s0)

    def pair(it, m8):
        a = 2 * it + 1
        b = a + 1
        qs_arrival(b).wait_recv()
        forward(b + 1)
        m8 = stage(a, s0, s1, m8)
        sib_merge(a - 1)
        pl.when(it >= 1)(lambda: y_send(a - 1).start())
        qs_arrival(b + 1).wait_recv()
        forward(b + 2)
        m8 = stage(b, s1, s0, m8)
        sib_merge(a)
        y_send(a).start()
        return m8

    m8 = lax.fori_loop(0, 2, pair, m8)
    qs_arrival(6).wait_recv()
    m8 = stage(5, s0, s1, m8)
    sib_merge(4)
    y_send(4).start()
    y_merge(0)
    stage(6, s1, None, m8)
    sib_merge(5)
    y_send(5).start()
    qs_arrival(7).wait_recv()
    m8 = all_scores(7, s0)
    sib_merge(6)
    y_send(6).start()
    stage(7, s0, None, m8)
    z_merge(0)
    sib_merge(7)
    y_merge(1)
    gather_y(0)
    for h in range(2):
        for i in range(1, NZ):
            qz(h, i).wait_send()
            if h == 0:
                z_send(0, i).wait_send()
    for s in range(8):
        qs(s).wait_send()
        sib_send(s).wait_send()
        if 1 <= s <= 6:
            qy_all(s).wait_send()
            y_send(s).wait_send()
    loads[6].wait()
    z_merge(1)
    gather_core(0)
    gather_y(1)
    part[...] = project(0)
    for h in range(2):
        for i in range(1, NZ):
            az(h, i).wait_send()
            if h == 1:
                z_send(1, i).wait_send()
    gather_core(1)
    part[...] += project(1)
    half[...] = part[...].astype(BF16)

    per = part.shape[0] // 4

    def mine(xx):
        return half.at[pl.ds(pl.multiple_of(xx * per, 32), per), :]

    def tp_send(i):
        to = (x + i) % 4
        return remote(mine(to), tpin.at[i], tp_s.at[i], tp_r.at[i], (k, to))

    for i in (2, 1, 3):
        tp_send(i).start()
    for h in range(2):
        for i in range(1, NY):
            ay_all(h, i).wait_send()
        for i in range(NY):
            a_sib(h, i).wait_send()
    total = part[pl.ds(pl.multiple_of(x * per, 8), per), :]
    for i in range(1, 4):
        tp_send(i).wait_recv()
        total = total + tpin[i].astype(F32)
    out_ref[...] = total.astype(BF16)
    for i in range(1, 4):
        tp_send(i).wait_send()


def per_device(queries, keys, values, kept, suffix_keys, suffix_values, lengths, out_weight):
    any_space = pl.BlockSpec(memory_space=pl.ANY)
    vmem = pl.BlockSpec(memory_space=pltpu.VMEM)
    sem = pltpu.SemaphoreType.DMA
    return pl.pallas_call(
        kernel,
        out_shape=jax.ShapeDtypeStruct((96, 128), BF16),
        in_specs=[
            vmem, any_space, any_space, vmem, any_space, any_space,
            pl.BlockSpec(memory_space=pltpu.SMEM), any_space,
        ],
        out_specs=vmem,
        scratch_shapes=[
            pltpu.VMEM((2, KEYS, HD), BF16),
            pltpu.VMEM((2, KEYS, HD), BF16),
            pltpu.VMEM((2, VR, KEYS), BF16),
            pltpu.VMEM((KEYS, HD), BF16),
            pltpu.VMEM((KEYS, UNIT), F32),
            pltpu.VMEM((KEYS, UNIT), F32),
            pltpu.VMEM((ROWS, SPAN, 2 * HD), BF16),
            pltpu.VMEM((ROWS, SPAN, 2 * HD), BF16),
            pltpu.VMEM((2 * G * HD, 128), BF16),
            pltpu.VMEM((2, QV, HD), F32),
            pltpu.VMEM((2, NY, 2, NZ, QV, HD), BF16),
            pltpu.VMEM((8, 2, VR, HALF), BF16),
            pltpu.VMEM((8, VR, HALF), BF16),
            pltpu.VMEM((8, VR, HALF), BF16),
            pltpu.VMEM((8, VR, HALF), BF16),
            pltpu.VMEM((2, NZ, QV + 16, HD), BF16),
            pltpu.VMEM((2, NZ, QV + 16, HD), BF16),
            pltpu.VMEM((2, NZ, NY, 2, QV, HD), BF16),
            pltpu.VMEM((NZ * NY * 2 * QV, HD), F32),
            pltpu.VMEM((2, QV, HD), F32),
            pltpu.VMEM((2, QV, HD), F32),
            pltpu.VMEM((384, 128), F32),
            pltpu.VMEM((384, 128), BF16),
            pltpu.VMEM((4, 96, 128), BF16),
            sem((7,)),
            sem((2, 8)), sem((2, 8)), sem((8,)), sem((8,)), sem((8,)), sem((8,)),
            sem((8,)), sem((8,)), sem((8,)), sem((8,)), sem((2, 8)), sem((2, 8)),
            sem((2, 8)), sem((2, 8)), sem((2, 4)), sem((2, 4)), sem((2, 4)), sem((2, 4)),
            sem((4,)), sem((4,)),
        ],
        compiler_params=pltpu.CompilerParams(
            collective_id=0, has_side_effects=True, vmem_limit_bytes=60 * 2**20
        ),
    )(queries, keys, values, kept.reshape(-1, 128), suffix_keys, suffix_values, lengths, out_weight)


def solution(mesh):
    return jax.shard_map(
        per_device,
        mesh=mesh,
        in_specs=(
            P("kv", "tp"),
            P("kv", "tp"),
            P("kv", "tp"),
            P("kv"),
            P("kv", None, "tp"),
            P("kv", None, "tp"),
            P("kv"),
            P("tp", "kv"),
        ),
        out_specs=P("tp", "kv"),
        check_vma=False,
    )
```
